32 devices in a mesh: fsdp: 4 (over x, core), replica: 8 (over z, y).
Axes of the slice: x: 2, y: 2, z: 4, core: 2. Of those that a mesh axis runs over, the one named last changes fastest.
Arguments:
- weights: float32 [32, 512, 2048], P('replica', 'fsdp'), may hold values from -0.125 to 0.125
- momentum: bfloat16 [32, 512, 2048], P('replica', 'fsdp'), may hold values from -6 to 6
- tokens: bfloat16 [28672, 2048], P(('fsdp', 'replica')), may hold values from -6 to 6
- block_expert: int32 [224], P(('fsdp', 'replica')), may hold values from 0 to 31, as said below
- owner_expert: int32 [32], replicated, may hold values from 0 to 31, as said below
Outputs:
- fresh: bfloat16 [32, 512, 2048], P(('fsdp', 'replica'))
- rollout: bfloat16 [28672, 512], P(('fsdp', 'replica'))
The draws below stay inside these ranges and needn't reach their ends.
Inputs may be any that keep to these rules, and one draw needn't show every extreme that they name: `owner_expert`: within each group g the entries g * N to g * N + N - 1 (N the fsdp axis size) are a permutation of the expert numbers g * N to g * N + N - 1. `block_expert`: the blocks of the device at fsdp index f and replica index r are blocks (f * R + r) * 7 to (f * R + r) * 7 + 7 - 1 (R the replica axis size). Each names an expert that owner_expert assigns to fsdp index f; the 7 blocks of one device name experts of distinct groups; in every fsdp index one group is named by every device of that index.
All inputs are finite; a program needn't handle non-finite values.
Results may differ from the reference program's by a relative error of at most 0.008.
Values may be sent and summed in bfloat16 or wider, within the bound.
No kernel may reach another device: no remote copies, remote signals or barrier semaphores. Data moves between devices by JAX's collectives and lax.ppermute only.
A program may use at most 128 MiB of HBM per device.

```python
import math
import jax
import jax.numpy as jnp
from jax import lax

ROWS_E = 512
COLS = 2048
ITERS = 4
BLOCKS = 7
TOK_BLOCK = 128
EXPERTS = 32
ROLL = 28672
NBLOCK = 224
N_FSDP = 4
N_REPLICA = 8


def owner_table(key):
    keys = jax.random.split(jax.random.fold_in(key, 11), N_REPLICA)
    perms = jax.vmap(lambda k: jax.random.permutation(k, N_FSDP))(keys)
    offsets = N_FSDP * jnp.arange(N_REPLICA, dtype=jnp.int32)[:, None]
    return (perms.astype(jnp.int32) + offsets).reshape(-1).astype(jnp.int32)


def draw_owner_expert(key, part):
    return owner_table(key)


def draw_block_expert(key, part):
    table = owner_table(key).reshape(N_REPLICA, N_FSDP)
    base = jax.random.fold_in(key, 23)
    hottest = jax.random.randint(jax.random.fold_in(base, 1), (N_FSDP,), 0, N_REPLICA)

    def single(device):
        column = device // N_REPLICA
        dev_key = jax.random.fold_in(base, device + 2)
        favored = hottest[column]
        others = (favored + 1 + jax.random.permutation(jax.random.fold_in(dev_key, 1), N_REPLICA - 1)) % N_REPLICA
        chosen = jnp.concatenate([favored[None], others[:BLOCKS - 1]])
        chosen = chosen[jax.random.permutation(jax.random.fold_in(dev_key, 2), BLOCKS)]
        return table[chosen, column]
    devices = jnp.arange(N_FSDP * N_REPLICA, dtype=jnp.int32)
    return jax.vmap(single)(devices).reshape(-1).astype(jnp.int32)


def draw_momentum(key, part):
    keys = jax.random.split(jax.random.fold_in(key, 31), 3)
    noise = jnp.clip(jax.random.normal(keys[0], (EXPERTS, ROWS_E, COLS), jnp.float32), -4.0, 4.0)
    row_scale = jnp.exp(jax.random.uniform(keys[1], (EXPERTS, ROWS_E, 1), jnp.float32) * math.log(10.0))
    col_scale = jnp.exp(jax.random.uniform(keys[2], (EXPERTS, 1, COLS), jnp.float32) * math.log(10.0))
    return (0.01 * noise * row_scale * col_scale).astype(jnp.bfloat16)


def block_levels(own_key, shape, pieces, low, largest):
    def one(dim, parts):
        steps = jax.random.uniform(jax.random.fold_in(jax.random.fold_in(own_key, 6), dim), (parts,), jnp.float32, low / len(pieces), largest / len(pieces))
        return jnp.repeat(jnp.exp(steps), shape[dim] // parts).reshape((-1,) + (1,) * (len(shape) - dim - 1))

    factor_of = one(*pieces[0])
    for cut in pieces[1:]:
        factor_of = factor_of * one(*cut)
    return factor_of


def normal_values(rng, extent, deviation, most, pieces=(), kind=jnp.bfloat16):
    result = deviation * jax.random.normal(rng, extent, jnp.float32)
    if pieces:
        result = result * block_levels(rng, extent, pieces, -0.22, 0.18)
    return jnp.clip(result, -most, most).astype(kind)


def setup_inputs(seed: int = 0) -> dict:
    streams_of = jax.random.split(jax.random.key(seed), 6)
    weights = normal_values(streams_of[0], (EXPERTS, ROWS_E, COLS), COLS ** -0.5, 0.125, ((0, 8), (1, 4)), jnp.float32)
    momentum = draw_momentum(jax.random.fold_in(streams_of[5], 71), 0)
    tokens = normal_values(streams_of[2], (ROLL, COLS), 1.0, 6.0, ((0, 32),))
    block_expert = draw_block_expert(jax.random.fold_in(streams_of[5], 71), 0)
    owner_expert = draw_owner_expert(jax.random.fold_in(streams_of[5], 71), 0)
    return {"weights": weights, "momentum": momentum, "tokens": tokens, "block_expert": block_expert, "owner_expert": owner_expert}


quintic_one = 3.4445
quintic_two = -4.775
quintic_three = 2.0315
learn_rate = 0.05
weight_decay = 0.1
norm_eps = 1e-07

def orthogonalize(moment):
    wide = moment.astype(jnp.float32)
    state = (wide / (jnp.sqrt(jnp.sum(wide * wide)) + norm_eps)).astype(jnp.bfloat16)
    for _ in range(ITERS):
        current = state.astype(jnp.float32)
        square = jnp.dot(current, current.T, precision=lax.Precision.HIGHEST).astype(jnp.bfloat16)
        sq_wide = square.astype(jnp.float32)
        poly = (quintic_two * sq_wide + quintic_three * jnp.dot(sq_wide, sq_wide, precision=lax.Precision.HIGHEST)).astype(jnp.bfloat16)
        state = (quintic_one * current + jnp.dot(poly.astype(jnp.float32), current, precision=lax.Precision.HIGHEST)).astype(jnp.bfloat16)
    return state

def reference(weights, momentum, tokens, block_expert, owner_expert):
    factor = learn_rate * 0.2 * math.sqrt(max(ROWS_E, COLS))

    def refresh(index):
        update = orthogonalize(momentum[index]).astype(jnp.float32)
        return (weights[index] * (1.0 - learn_rate * weight_decay) - factor * update).astype(jnp.bfloat16)
    new_weight = lax.map(refresh, jnp.arange(EXPERTS, dtype=jnp.int32))
    slots = jnp.arange(EXPERTS, dtype=jnp.int32)
    fsdp_pos = slots // N_REPLICA
    rep_pos = slots % N_REPLICA
    order = owner_expert[rep_pos * N_FSDP + fsdp_pos]
    fresh = new_weight[order]
    blocks = tokens.reshape(NBLOCK, TOK_BLOCK, COLS)

    def serve(pair):
        rows, expert = pair
        matrix = new_weight[expert].astype(jnp.float32)
        return jnp.dot(rows.astype(jnp.float32), matrix.T, precision=lax.Precision.HIGHEST).astype(jnp.bfloat16)
    rollout = lax.map(serve, (blocks, block_expert)).reshape(ROLL, ROWS_E)
    return (fresh, rollout)
```

```python
import functools
import math

import jax
import jax.numpy as jnp
from jax import lax
from jax.experimental import pallas as pl
from jax.experimental.pallas import tpu as pltpu
from jax.sharding import PartitionSpec as P

ITERS = 4


quintic_one = 3.4445
quintic_two = -4.775
quintic_three = 2.0315
learn_rate = 0.05
weight_decay = 0.1
norm_eps = 1e-07

ROW_BY_ROW = (((1,), (1,)), ((), ()))
ANY = pl.BlockSpec(memory_space=pl.ANY)
SMEM = pl.BlockSpec(memory_space=pltpu.SMEM)
VMEM = pl.BlockSpec(memory_space=pltpu.VMEM)


def partner(index, step, size):
    if size & (size - 1) == 0:
        return index ^ step
    return (index + step) % size


def source(index, step, size):
    if size & (size - 1) == 0:
        return index ^ step
    return (index + size - step) % size


def send(value, axis, step, size):
    return lax.ppermute(value, axis, [(i, partner(i, step, size)) for i in range(size)])


def send_back(value, axis, step, size):
    return lax.ppermute(value, axis, [(partner(i, step, size), i) for i in range(size)])


def far_first(size):
    half = size // 2
    evens = list(range(half, size, 2))
    odds = list(range(half + 1, size, 2))
    return evens + odds + list(range(half - 1, 0, -1))


def after(value, *others):
    return lax.optimization_barrier((value, *others))[0]


def pick_kernel(count, array_ref, index_ref, *rest):
    outs, sem = rest[-count - 1 : -1], rest[-1]
    copies = [
        pltpu.make_async_copy(array_ref.at[index_ref[k]], outs[k], sem.at[k])
        for k in range(count)
    ]
    for copy in copies:
        copy.start()
    for copy in copies:
        copy.wait()


def pick(array, index, count, *later_than):
    shape = array.shape[1:]
    size = math.prod(shape) * array.dtype.itemsize * count
    return pl.pallas_call(
        functools.partial(pick_kernel, count),
        out_shape=[jax.ShapeDtypeStruct(shape, array.dtype)] * count,
        in_specs=[ANY, SMEM] + [ANY] * len(later_than),
        out_specs=[VMEM] * count,
        scratch_shapes=[pltpu.SemaphoreType.DMA((count,))],
        cost_estimate=pl.CostEstimate(flops=0, bytes_accessed=2 * size, transcendentals=0),
        name="pick",
    )(array, index, *later_than)


def newton_kernel(chunk, place_ref, *rest):
    pieces, out_ref, poly_ref = rest[:-2], rest[-2], rest[-1]
    shard, width = pieces[0].shape
    total = jnp.float32(0.0)
    for piece in pieces:
        wide = piece[...].astype(jnp.float32)
        total += jnp.sum(wide * wide)
    scale = 1.0 / (jnp.sqrt(total) + norm_eps)
    for k, piece in enumerate(pieces):
        at = pl.ds(pl.multiple_of(place_ref[k] * shard, shard), shard)
        out_ref[at, :] = (piece[...].astype(jnp.float32) * scale).astype(jnp.bfloat16)

    def iteration(_, carry):
        state = out_ref[...]
        square = lax.dot_general(
            state, state, ROW_BY_ROW, preferred_element_type=jnp.float32
        ).astype(jnp.bfloat16)
        twice = jnp.dot(square, square, preferred_element_type=jnp.float32)
        poly_ref[...] = (
            quintic_two * square.astype(jnp.float32) + quintic_three * twice
        ).astype(jnp.bfloat16)

        def columns(c, carry):
            at = pl.ds(pl.multiple_of(c * chunk, chunk), chunk)
            part = out_ref[:, at]
            out_ref[:, at] = (
                quintic_one * part.astype(jnp.float32)
                + jnp.dot(poly_ref[...], part, preferred_element_type=jnp.float32)
            ).astype(jnp.bfloat16)
            return carry

        return lax.fori_loop(0, width // chunk, columns, carry)

    lax.fori_loop(0, ITERS, iteration, 0)


def orthogonalize(pieces, place):
    shard, width = pieces[0].shape
    rows = shard * len(pieces)
    chunk = 1024 if width % 1024 == 0 else width
    return pl.pallas_call(
        functools.partial(newton_kernel, chunk),
        out_shape=jax.ShapeDtypeStruct((rows, width), jnp.bfloat16),
        in_specs=[SMEM] + [VMEM] * len(pieces),
        out_specs=VMEM,
        scratch_shapes=[
            pltpu.VMEM((rows, rows), jnp.bfloat16),
        ],
        compiler_params=pltpu.CompilerParams(vmem_limit_bytes=40 << 20),
        cost_estimate=pl.CostEstimate(
            flops=ITERS * 2 * rows * rows * (2 * width + rows),
            bytes_accessed=4 * rows * width,
            transcendentals=0,
        ),
        name="newton",
    )(place, *pieces)


def per_device(weights, momentum, tokens, block_expert, owner_expert):
    owners = lax.axis_size("fsdp")
    groups = lax.axis_size("replica")
    group = lax.axis_index("replica")
    column = lax.axis_index("fsdp")
    blocks = block_expert.shape[0]
    width = tokens.shape[1]
    shard = weights.shape[1]
    rows = shard * owners
    resident = tokens.reshape(blocks, -1, width)
    target = block_expert // owners
    far = far_first(groups)
    steps = jnp.array(far + [0], jnp.int32)
    served = partner(group, steps, groups)
    slot = jnp.sum(
        jnp.where(
            target[None, :] == served[:, None], jnp.arange(blocks, dtype=jnp.int32)[None, :], 0
        ),
        axis=1,
    )
    table = lax.dynamic_slice_in_dim(owner_expert, group * owners, owners, 0) - group * owners
    near = list(range(owners - 1, -1, -1))
    near_steps = jnp.array(near, jnp.int32)
    local = table[partner(column, near_steps, owners)]
    place = source(column, near_steps, owners)

    arrived = {}
    first = pick(resident, slot[:2], 2)
    for k in range(2):
        arrived[k] = send(first[k], "replica", far[k], groups)
    parts = pick(momentum, local, owners)
    moment = [send(parts[k], "fsdp", near[k], owners) for k in range(owners - 1)] + [parts[-1]]

    second = pick(resident, slot[2:4], 2, *moment[:2])
    for k in range(2):
        arrived[2 + k] = send(second[k], "replica", far[2 + k], groups)
    kept = 1.0 - learn_rate * weight_decay
    decayed = [
        (lax.dynamic_index_in_dim(weights, local[k], 0, keepdims=False) * kept).astype(jnp.bfloat16)
        for k in range(owners)
    ]
    master = [send(after(decayed[k], *moment[:2]), "fsdp", near[k], owners) for k in range(owners - 1)]
    master.append(decayed[-1])
    update = orthogonalize(moment, place)
    third = pick(resident, slot[4:], groups - 4, master[0])
    for k in range(4, groups - 1):
        arrived[k] = send(third[k - 4], "replica", far[k], groups)
    arrived[groups - 1] = third[-1]

    whole = jnp.zeros((rows, width), jnp.bfloat16)
    for k in range(owners):
        whole = lax.dynamic_update_slice_in_dim(whole, master[k], place[k] * shard, 0)
    factor = learn_rate * 0.2 * math.sqrt(max(rows, width))
    refreshed = (
        whole.astype(jnp.float32) - factor * update.astype(jnp.float32)
    ).astype(jnp.bfloat16)
    fresh = refreshed[None]

    def product(block):
        return lax.dot_general(
            block, refreshed, ROW_BY_ROW, preferred_element_type=jnp.float32
        ).astype(jnp.bfloat16)

    answers = [
        send_back(product(arrived[k]), "replica", far[k], groups) for k in range(groups - 1)
    ]
    answers.append(product(arrived[groups - 1]))
    order = jnp.argmax(target[:, None] == served[None, :], axis=1)
    rollout = jnp.take(jnp.stack(answers), order, axis=0, mode="clip").reshape(-1, rows)
    return (fresh, rollout)


def solution(mesh):
    placed = (
        P("replica", "fsdp", None),
        P("replica", "fsdp", None),
        P(("fsdp", "replica"), None),
        P(("fsdp", "replica")),
        P(),
    )
    return jax.shard_map(
        per_device,
        mesh=mesh,
        in_specs=placed,
        out_specs=(P(("fsdp", "replica"), None, None), P(("fsdp", "replica"), None)),
        check_vma=False,
    )
```

```python
import functools
import math

import jax
import jax.numpy as jnp
from jax import lax
from jax.experimental import pallas as pl
from jax.experimental.pallas import tpu as pltpu
from jax.sharding import PartitionSpec as P

ITERS = 4


quintic_one = 3.4445
quintic_two = -4.775
quintic_three = 2.0315
learn_rate = 0.05
weight_decay = 0.1
norm_eps = 1e-07

ROW_BY_ROW = (((1,), (1,)), ((), ()))
ANY = pl.BlockSpec(memory_space=pl.ANY)
SMEM = pl.BlockSpec(memory_space=pltpu.SMEM)
VMEM = pl.BlockSpec(memory_space=pltpu.VMEM)


def partner(index, step, size):
    if size & (size - 1) == 0:
        return index ^ step
    return (index + step) % size


def source(index, step, size):
    if size & (size - 1) == 0:
        return index ^ step
    return (index + size - step) % size


def send(value, axis, step, size):
    return lax.ppermute(value, axis, [(i, partner(i, step, size)) for i in range(size)])


def send_back(value, axis, step, size):
    return lax.ppermute(value, axis, [(partner(i, step, size), i) for i in range(size)])


def after(value, *others):
    return lax.optimization_barrier((value, *others))[0]


def pick_blocks_kernel(steps, groups, owners, tokens_ref, named_ref, *rest):
    outs, sem = rest[-1 - len(steps) : -1], rest[-1]
    group = lax.axis_index("replica")
    copies = []
    for k, step in enumerate(steps):
        wanted = partner(group, step, groups)
        slot = jnp.int32(0)
        for b in range(tokens_ref.shape[0]):
            slot = jnp.where(lax.div(named_ref[b], jnp.int32(owners)) == wanted, b, slot)
        copies.append(pltpu.make_async_copy(tokens_ref.at[slot], outs[k], sem.at[k]))
    for copy in copies:
        copy.start()
    for copy in copies:
        copy.wait()


def pick_blocks(resident, named, steps, groups, owners, *later_than):
    shape = resident.shape[1:]
    size = math.prod(shape) * resident.dtype.itemsize * len(steps)
    return pl.pallas_call(
        functools.partial(pick_blocks_kernel, steps, groups, owners),
        out_shape=[jax.ShapeDtypeStruct(shape, resident.dtype)] * len(steps),
        in_specs=[ANY, SMEM] + [ANY] * len(later_than),
        out_specs=[VMEM] * len(steps),
        scratch_shapes=[pltpu.SemaphoreType.DMA((len(steps),))],
        compiler_params=pltpu.CompilerParams(vmem_limit_bytes=56 << 20),
        cost_estimate=pl.CostEstimate(flops=0, bytes_accessed=2 * size, transcendentals=0),
        name="pick_blocks",
    )(resident, named, *later_than)


def block_of(group, named_ref, blocks, owners):
    slot = jnp.int32(0)
    for b in range(blocks):
        slot = jnp.where(lax.div(named_ref[b], jnp.int32(owners)) == group, b, slot)
    return slot


def lead_kernel(steps, groups, owners, tokens_ref, moment_ref, named_ref, owner_ref, *rest):
    outs, moment_out, sem = rest[: len(steps)], rest[-2], rest[-1]
    group = lax.axis_index("replica")
    first = group * owners
    copies = []
    for k, step in enumerate(steps):
        slot = block_of(partner(group, step, groups), named_ref, tokens_ref.shape[0], owners)
        copies.append(pltpu.make_async_copy(tokens_ref.at[slot], outs[k], sem.at[k]))
        copies[-1].start()
    for p in range(owners):
        copies.append(
            pltpu.make_async_copy(
                moment_ref.at[owner_ref[first + p] - first], moment_out.at[p], sem.at[len(steps) + p]
            )
        )
        copies[-1].start()
    for copy in copies:
        copy.wait()


def lead_pick(resident, momentum, named, owner_expert, steps, groups):
    owners = momentum.shape[0]
    shape = resident.shape[1:]
    out = pl.pallas_call(
        functools.partial(lead_kernel, steps, groups, owners),
        out_shape=[jax.ShapeDtypeStruct(shape, resident.dtype)] * len(steps)
        + [jax.ShapeDtypeStruct(momentum.shape, momentum.dtype)],
        in_specs=[ANY, ANY, SMEM, SMEM],
        out_specs=[VMEM] * (1 + len(steps)),
        scratch_shapes=[pltpu.SemaphoreType.DMA((len(steps) + owners,))],
        compiler_params=pltpu.CompilerParams(vmem_limit_bytes=56 << 20),
        cost_estimate=pl.CostEstimate(
            flops=0, bytes_accessed=4 * (momentum.size + len(steps) * math.prod(shape)), transcendentals=0
        ),
        name="lead_pick",
    )(resident, momentum, named, owner_expert)
    return out[:-1], out[-1]


def by_owner_kernel(owners, scale, later, array_ref, owner_ref, *rest):
    out_ref, *scratch = rest[later:]
    held, sem = (out_ref, scratch[0]) if scale is None else scratch
    first = lax.axis_index("replica") * owners
    copies = [
        pltpu.make_async_copy(array_ref.at[owner_ref[first + p] - first], held.at[p], sem.at[p])
        for p in range(owners)
    ]
    for copy in copies:
        copy.start()
    for p, copy in enumerate(copies):
        copy.wait()
        if scale is not None:
            out_ref[p] = (held[p] * scale).astype(out_ref.dtype)


def by_owner(array, owner_expert, scale, *later_than):
    owners = array.shape[0]
    scratch = [pltpu.SemaphoreType.DMA((owners,))]
    if scale is not None:
        scratch = [pltpu.VMEM(array.shape, array.dtype)] + scratch
    return pl.pallas_call(
        functools.partial(by_owner_kernel, owners, scale, len(later_than)),
        out_shape=jax.ShapeDtypeStruct(array.shape, jnp.bfloat16),
        in_specs=[ANY, SMEM] + [ANY] * len(later_than),
        out_specs=VMEM,
        scratch_shapes=scratch,
        compiler_params=pltpu.CompilerParams(vmem_limit_bytes=56 << 20),
        cost_estimate=pl.CostEstimate(
            flops=0, bytes_accessed=array.size * (array.dtype.itemsize + 2), transcendentals=0
        ),
        name="by_owner",
    )(array, owner_expert, *later_than)


def newton_kernel(chunk, moment_ref, *rest):
    out_ref, poly_ref = rest[-2:]
    width = moment_ref.shape[1]
    wide = moment_ref[...].astype(jnp.float32)
    scale = 1.0 / (jnp.sqrt(jnp.sum(wide * wide)) + norm_eps)
    out_ref[...] = (moment_ref[...].astype(jnp.float32) * scale).astype(jnp.bfloat16)

    def iteration(_, carry):
        state = out_ref[...]
        square = lax.dot_general(
            state, state, ROW_BY_ROW, preferred_element_type=jnp.float32
        ).astype(jnp.bfloat16)
        twice = jnp.dot(square, square, preferred_element_type=jnp.float32)
        poly_ref[...] = (
            quintic_two * square.astype(jnp.float32) + quintic_three * twice
        ).astype(jnp.bfloat16)

        def columns(c, carry):
            at = pl.ds(pl.multiple_of(c * chunk, chunk), chunk)
            part = out_ref[:, at]
            out_ref[:, at] = (
                quintic_one * part.astype(jnp.float32)
                + jnp.dot(poly_ref[...], part, preferred_element_type=jnp.float32)
            ).astype(jnp.bfloat16)
            return carry

        return lax.fori_loop(0, width // chunk, columns, carry)

    lax.fori_loop(0, ITERS, iteration, 0)


def orthogonalize(moment, *later_than):
    rows, width = moment.shape
    chunk = 1024 if width % 1024 == 0 else width
    return pl.pallas_call(
        functools.partial(newton_kernel, chunk),
        out_shape=jax.ShapeDtypeStruct((rows, width), jnp.bfloat16),
        in_specs=[VMEM] + [ANY] * len(later_than),
        out_specs=VMEM,
        scratch_shapes=[pltpu.VMEM((rows, rows), jnp.bfloat16)],
        compiler_params=pltpu.CompilerParams(vmem_limit_bytes=56 << 20),
        cost_estimate=pl.CostEstimate(
            flops=ITERS * 2 * rows * rows * (2 * width + rows),
            bytes_accessed=4 * rows * width,
            transcendentals=0,
        ),
        name="newton",
    )(moment, *later_than)


def refresh_kernel(factor, update_ref, master_ref, *rest):
    rest[-1][...] = (
        master_ref[...].astype(jnp.float32) - factor * update_ref[...].astype(jnp.float32)
    ).astype(jnp.bfloat16)


def refresh(update, master, *later_than):
    factor = learn_rate * 0.2 * math.sqrt(max(update.shape))
    return pl.pallas_call(
        functools.partial(refresh_kernel, factor),
        out_shape=jax.ShapeDtypeStruct(update.shape, jnp.bfloat16),
        in_specs=[VMEM] * 2 + [ANY] * len(later_than),
        out_specs=VMEM,
        compiler_params=pltpu.CompilerParams(vmem_limit_bytes=32 << 20),
        cost_estimate=pl.CostEstimate(
            flops=2 * update.size, bytes_accessed=6 * update.size, transcendentals=0
        ),
        name="refresh",
    )(update, master, *later_than)


def per_device(weights, momentum, tokens, block_expert, owner_expert):
    owners = lax.axis_size("fsdp")
    groups = lax.axis_size("replica")
    group = lax.axis_index("replica")
    blocks = block_expert.shape[0]
    width = tokens.shape[1]
    rows = weights.shape[1] * owners
    resident = tokens.reshape(blocks, -1, width)
    half = groups // 2
    far = list(range(half, groups, 2)) + list(range(half + 1, groups, 2))
    near = list(range(1, half))
    arrived = {}

    def pick(chosen, *later_than):
        return pick_blocks(resident, block_expert, chosen, groups, owners, *later_than)

    def send_all(blocks, chosen):
        for block, step in zip(blocks, chosen):
            arrived[step] = send(block, "replica", step, groups)

    lead, trail = far[: half // 2], far[half // 2 :]
    first, outgoing = lead_pick(resident, momentum, block_expert, owner_expert, lead, groups)
    send_all(first, lead)
    moment = lax.all_to_all(outgoing, "fsdp", 0, 0, tiled=True)
    second = pick(near, first[0])
    send_all(second, near)
    third = pick(trail + [0], arrived[near[0]])
    send_all(third, trail)
    arrived[0] = third[-1]
    kept = 1.0 - learn_rate * weight_decay
    master = lax.all_to_all(by_owner(weights, owner_expert, kept, moment), "fsdp", 0, 0, tiled=True)
    update = orthogonalize(moment.reshape(rows, width), third[0], *[arrived[step] for step in near])
    refreshed = refresh(update, master.reshape(rows, width), *[arrived[step] for step in lead])

    def product(block):
        return lax.dot_general(
            block, refreshed, ROW_BY_ROW, preferred_element_type=jnp.float32
        ).astype(jnp.bfloat16)

    answer = {0: product(arrived[0])}
    for step in near + lead + trail:
        answer[step] = send_back(product(arrived[step]), "replica", step, groups)
    steps = list(answer)
    served = partner(group, jnp.array(steps, jnp.int32), groups)
    order = jnp.argmax((block_expert // owners)[:, None] == served[None, :], axis=1)
    answers = jnp.stack([answer[step] for step in steps])
    rollout = jnp.take(answers, order, axis=0, mode="clip").reshape(-1, rows)
    return (refreshed[None], rollout)


def solution(mesh):
    placed = (
        P("replica", "fsdp", None),
        P("replica", "fsdp", None),
        P(("fsdp", "replica"), None),
        P(("fsdp", "replica")),
        P(),
    )
    return jax.shard_map(
        per_device,
        mesh=mesh,
        in_specs=placed,
        out_specs=(P(("fsdp", "replica"), None, None), P(("fsdp", "replica"), None)),
        check_vma=False,
    )
```

```python
import functools
import math

import jax
import jax.numpy as jnp
from jax import lax
from jax.experimental import pallas as pl
from jax.experimental.pallas import tpu as pltpu
from jax.sharding import PartitionSpec as P

ITERS = 4


quintic_one = 3.4445
quintic_two = -4.775
quintic_three = 2.0315
learn_rate = 0.05
weight_decay = 0.1
norm_eps = 1e-07

ROW_BY_ROW = (((1,), (1,)), ((), ()))
ANY = pl.BlockSpec(memory_space=pl.ANY)
SMEM = pl.BlockSpec(memory_space=pltpu.SMEM)
VMEM = pl.BlockSpec(memory_space=pltpu.VMEM)


def partner(index, step, size):
    if size & (size - 1) == 0:
        return index ^ step
    return (index + step) % size


def source(index, step, size):
    if size & (size - 1) == 0:
        return index ^ step
    return (index + size - step) % size


def send(value, axis, step, size):
    return lax.ppermute(value, axis, [(i, partner(i, step, size)) for i in range(size)])


def send_back(value, axis, step, size):
    return lax.ppermute(value, axis, [(partner(i, step, size), i) for i in range(size)])


def after(value, *others):
    return lax.optimization_barrier((value, *others))[0]


def block_of(group, named_ref, blocks, owners):
    slot = jnp.int32(0)
    for b in range(blocks):
        slot = jnp.where(lax.div(named_ref[b], jnp.int32(owners)) == group, b, slot)
    return slot


def pick_kernel(wanted, owners, tokens_ref, named_ref, *rest):
    outs, sem = rest[-1 - len(wanted) : -1], rest[-1]
    if rest[-2].ndim == 3:
        outs = [rest[-2].at[k] for k in range(len(wanted))]
    copies = []
    for k, group_of in enumerate(wanted):
        slot = block_of(group_of(), named_ref, tokens_ref.shape[0], owners)
        copies.append(pltpu.make_async_copy(tokens_ref.at[slot], outs[k], sem.at[k]))
        copies[-1].start()
    for copy in copies:
        copy.wait()


def pick(resident, named, wanted, owners, stacked, *later_than):
    shape = resident.shape[1:]
    size = math.prod(shape) * resident.dtype.itemsize * len(wanted)
    if stacked:
        out_shape = jax.ShapeDtypeStruct((len(wanted),) + shape, resident.dtype)
    else:
        out_shape = [jax.ShapeDtypeStruct(shape, resident.dtype)] * len(wanted)
    return pl.pallas_call(
        functools.partial(pick_kernel, wanted, owners),
        out_shape=out_shape,
        in_specs=[ANY, SMEM] + [ANY] * len(later_than),
        out_specs=VMEM if stacked else [VMEM] * len(wanted),
        scratch_shapes=[pltpu.SemaphoreType.DMA((len(wanted),))],
        compiler_params=pltpu.CompilerParams(vmem_limit_bytes=56 << 20),
        cost_estimate=pl.CostEstimate(flops=0, bytes_accessed=2 * size, transcendentals=0),
        name="pick",
    )(resident, named, *later_than)


def by_owner_kernel(owners, scale, later, array_ref, owner_ref, *rest):
    outs, scratch = rest[later : later + owners], rest[later + owners :]
    held, sem = (outs, scratch[0]) if scale is None else scratch
    first = lax.axis_index("replica") * owners
    column = lax.axis_index("fsdp")
    copies = []
    for k in range(owners):
        expert = owner_ref[first + partner(column, k, owners)] - first
        target = outs[k] if scale is None else held.at[k]
        copies.append(pltpu.make_async_copy(array_ref.at[expert], target, sem.at[k]))
    for copy in copies:
        copy.start()
    for k, copy in enumerate(copies):
        copy.wait()
        if scale is not None:
            outs[k][...] = (held[k] * scale).astype(outs[k].dtype)


def by_owner(array, owner_expert, scale, *later_than):
    owners = array.shape[0]
    scratch = [pltpu.SemaphoreType.DMA((owners,))]
    if scale is not None:
        scratch = [pltpu.VMEM(array.shape, array.dtype)] + scratch
    return pl.pallas_call(
        functools.partial(by_owner_kernel, owners, scale, len(later_than)),
        out_shape=[jax.ShapeDtypeStruct(array.shape[1:], jnp.bfloat16)] * owners,
        in_specs=[ANY, SMEM] + [ANY] * len(later_than),
        out_specs=[VMEM] * owners,
        scratch_shapes=scratch,
        compiler_params=pltpu.CompilerParams(vmem_limit_bytes=56 << 20),
        cost_estimate=pl.CostEstimate(
            flops=0, bytes_accessed=array.size * (array.dtype.itemsize + 2), transcendentals=0
        ),
        name="by_owner",
    )(array, owner_expert, *later_than)


def newton_kernel(chunk, owners, *rest):
    pieces, (out_ref, poly_ref) = rest[:owners], rest[-2:]
    shard, width = pieces[0].shape
    column = lax.axis_index("fsdp")
    total = jnp.float32(0.0)
    for piece in pieces:
        wide = piece[...].astype(jnp.float32)
        total += jnp.sum(wide * wide)
    scale = 1.0 / (jnp.sqrt(total) + norm_eps)
    for step, piece in enumerate(pieces):
        start = source(column, step, owners) * shard
        out_ref[pl.ds(pl.multiple_of(start, shard), shard), :] = (
            piece[...].astype(jnp.float32) * scale
        ).astype(jnp.bfloat16)

    def iteration(_, carry):
        state = out_ref[...]
        square = lax.dot_general(
            state, state, ROW_BY_ROW, preferred_element_type=jnp.float32
        ).astype(jnp.bfloat16)
        twice = jnp.dot(square, square, preferred_element_type=jnp.float32)
        poly_ref[...] = (
            quintic_two * square.astype(jnp.float32) + quintic_three * twice
        ).astype(jnp.bfloat16)

        def columns(c, carry):
            at = pl.ds(pl.multiple_of(c * chunk, chunk), chunk)
            part = out_ref[:, at]
            out_ref[:, at] = (
                quintic_one * part.astype(jnp.float32)
                + jnp.dot(poly_ref[...], part, preferred_element_type=jnp.float32)
            ).astype(jnp.bfloat16)
            return carry

        return lax.fori_loop(0, width // chunk, columns, carry)

    lax.fori_loop(0, ITERS, iteration, 0)


def orthogonalize(pieces, *later_than):
    owners = len(pieces)
    rows, width = pieces[0].shape[0] * owners, pieces[0].shape[1]
    chunk = 1024 if width % 1024 == 0 else width
    return pl.pallas_call(
        functools.partial(newton_kernel, chunk, owners),
        out_shape=jax.ShapeDtypeStruct((rows, width), jnp.bfloat16),
        in_specs=[VMEM] * owners + [ANY] * len(later_than),
        out_specs=VMEM,
        scratch_shapes=[pltpu.VMEM((rows, rows), jnp.bfloat16)],
        compiler_params=pltpu.CompilerParams(vmem_limit_bytes=56 << 20),
        cost_estimate=pl.CostEstimate(
            flops=ITERS * 2 * rows * rows * (2 * width + rows),
            bytes_accessed=4 * rows * width,
            transcendentals=0,
        ),
        name="newton",
    )(*pieces, *later_than)


def refresh_kernel(factor, owners, update_ref, *rest):
    pieces, out_ref = rest[:owners], rest[-1]
    shard = pieces[0].shape[0]
    column = lax.axis_index("fsdp")
    for step, piece in enumerate(pieces):
        at = pl.ds(pl.multiple_of(source(column, step, owners) * shard, shard), shard)
        out_ref[at, :] = (
            piece[...].astype(jnp.float32) - factor * update_ref[at, :].astype(jnp.float32)
        ).astype(jnp.bfloat16)


def refresh(update, pieces, *later_than):
    factor = learn_rate * 0.2 * math.sqrt(max(update.shape))
    return pl.pallas_call(
        functools.partial(refresh_kernel, factor, len(pieces)),
        out_shape=jax.ShapeDtypeStruct(update.shape, jnp.bfloat16),
        in_specs=[VMEM] * (1 + len(pieces)) + [ANY] * len(later_than),
        out_specs=VMEM,
        compiler_params=pltpu.CompilerParams(vmem_limit_bytes=32 << 20),
        cost_estimate=pl.CostEstimate(
            flops=2 * update.size, bytes_accessed=6 * update.size, transcendentals=0
        ),
        name="refresh",
    )(update, *pieces, *later_than)


def per_device(weights, momentum, tokens, block_expert, owner_expert):
    owners = lax.axis_size("fsdp")
    groups = lax.axis_size("replica")
    group = lax.axis_index("replica")
    blocks = block_expert.shape[0]
    width = tokens.shape[1]
    rows = weights.shape[1] * owners
    resident = tokens.reshape(blocks, -1, width)
    half = groups // 2
    places = list(range(0, groups, 2))
    teams = [[team + place for place in places] for team in (0, 1)]
    far = list(range(half + 1, groups, 2))
    near = list(range(1, half, 2))

    def at_step(step):
        return lambda: partner(lax.axis_index("replica"), step, groups)

    def at_place(place):
        return lambda: lax.axis_index("replica") % 2 + place

    arrived = {}

    def pick_and_send(steps, *later_than):
        picked = pick(
            resident, block_expert, [at_step(step) for step in steps], owners, False, *later_than
        )
        for block, step in zip(picked, steps):
            arrived[step] = send(block, "replica", step, groups)
        return picked

    def exchange(blocks):
        return lax.all_to_all(blocks, "replica", 0, 0, axis_index_groups=teams, tiled=True)

    outgoing = pick(resident, block_expert, [at_place(place) for place in places], owners, True)
    team = exchange(outgoing)
    moment = by_owner(momentum, owner_expert, None, outgoing)
    moment = [moment[0]] + [send(moment[k], "fsdp", k, owners) for k in range(1, owners)]
    pick_and_send(near, outgoing)
    sent = pick_and_send(far, *moment, arrived[near[0]])
    kept = 1.0 - learn_rate * weight_decay
    master = by_owner(weights, owner_expert, kept, *moment )
    master = [master[0]] + [send(master[k], "fsdp", k, owners) for k in range(1, owners)]
    update = orthogonalize(moment , *[arrived[step] for step in near], sent[0])
    refreshed = refresh(update, master )

    def product(block):
        return lax.dot_general(
            block, refreshed, ROW_BY_ROW, preferred_element_type=jnp.float32
        ).astype(jnp.bfloat16)

    reply = product(team.reshape(-1, width)).reshape(half, -1, rows)
    answers = [exchange(reply)]
    steps = near + far
    replies = []
    for step in steps:
        replies.append(product(after(arrived[step], reply, *replies)))
        answers.append(send_back(replies[-1], "replica", step, groups)[None])
    served = jnp.concatenate(
        [
            group % 2 + jnp.array(places, jnp.int32),
            partner(group, jnp.array(steps, jnp.int32), groups),
        ]
    )
    order = jnp.argmax((block_expert // owners)[:, None] == served[None, :], axis=1)
    rollout = jnp.take(jnp.concatenate(answers), order, axis=0, mode="clip").reshape(-1, rows)
    return (refreshed[None], rollout)


def solution(mesh):
    placed = (
        P("replica", "fsdp", None),
        P("replica", "fsdp", None),
        P(("fsdp", "replica"), None),
        P(("fsdp", "replica")),
        P(),
    )
    return jax.shard_map(
        per_device,
        mesh=mesh,
        in_specs=placed,
        out_specs=(P(("fsdp", "replica"), None, None), P(("fsdp", "replica"), None)),
        check_vma=False,
    )
```

```python
import functools
import math

import jax
import jax.numpy as jnp
from jax import lax
from jax.experimental import pallas as pl
from jax.experimental.pallas import tpu as pltpu
from jax.sharding import PartitionSpec as P

ITERS = 4


quintic_one = 3.4445
quintic_two = -4.775
quintic_three = 2.0315
learn_rate = 0.05
weight_decay = 0.1
norm_eps = 1e-07

ROW_BY_ROW = (((1,), (1,)), ((), ()))
ANY = pl.BlockSpec(memory_space=pl.ANY)
SMEM = pl.BlockSpec(memory_space=pltpu.SMEM)
VMEM = pl.BlockSpec(memory_space=pltpu.VMEM)


def partner(index, step, size):
    if size & (size - 1) == 0:
        return index ^ step
    return (index + step) % size


def source(index, step, size):
    if size & (size - 1) == 0:
        return index ^ step
    return (index + size - step) % size


def send(value, axis, step, size):
    return lax.ppermute(value, axis, [(i, partner(i, step, size)) for i in range(size)])


def send_back(value, axis, step, size):
    return lax.ppermute(value, axis, [(partner(i, step, size), i) for i in range(size)])


def after(value, *others):
    return lax.optimization_barrier((value, *others))[0]


def block_of(group, named_ref, blocks, owners):
    slot = jnp.int32(0)
    for b in range(blocks):
        slot = jnp.where(lax.div(named_ref[b], jnp.int32(owners)) == group, b, slot)
    return slot


def pick_kernel(wanted, owners, tokens_ref, named_ref, *rest):
    held, sem, sent = rest[-3:]
    outs = rest[-3 - len(wanted) : -3]
    if len(rest[-4].shape) == 3:
        outs = [rest[-4].at[k] for k in range(len(wanted))]
    copies = []
    for k, group_of in enumerate(wanted):
        slot = block_of(group_of(), named_ref, tokens_ref.shape[0], owners)
        copies.append(pltpu.make_async_copy(tokens_ref.at[slot], held.at[k], sem.at[k]))
        copies[-1].start()
    leaving = []
    for k, copy in enumerate(copies):
        copy.wait()
        leaving.append(pltpu.make_async_copy(held.at[k], outs[k], sent.at[k]))
        leaving[-1].start()
    for copy in leaving:
        copy.wait()


def pick(resident, named, wanted, owners, stacked, *later_than):
    shape = resident.shape[1:]
    size = math.prod(shape) * resident.dtype.itemsize * len(wanted)
    if stacked:
        out_shape = jax.ShapeDtypeStruct((len(wanted),) + shape, resident.dtype)
    else:
        out_shape = [jax.ShapeDtypeStruct(shape, resident.dtype)] * len(wanted)
    return pl.pallas_call(
        functools.partial(pick_kernel, wanted, owners),
        out_shape=out_shape,
        in_specs=[ANY, SMEM] + [ANY] * len(later_than),
        out_specs=ANY if stacked else [ANY] * len(wanted),
        scratch_shapes=[pltpu.VMEM((len(wanted),) + shape, resident.dtype)]
        + [pltpu.SemaphoreType.DMA((len(wanted),))] * 2,
        compiler_params=pltpu.CompilerParams(vmem_limit_bytes=56 << 20),
        cost_estimate=pl.CostEstimate(flops=0, bytes_accessed=2 * size, transcendentals=0),
        name="pick",
    )(resident, named, *later_than)


def by_owner_kernel(owners, scale, later, array_ref, owner_ref, *rest):
    outs, scratch = rest[later : later + owners], rest[later + owners :]
    held, sem = (outs, scratch[0]) if scale is None else scratch
    first = lax.axis_index("replica") * owners
    column = lax.axis_index("fsdp")
    copies = []
    for k in range(owners):
        expert = owner_ref[first + partner(column, k, owners)] - first
        target = outs[k] if scale is None else held.at[k]
        copies.append(pltpu.make_async_copy(array_ref.at[expert], target, sem.at[k]))
    for copy in copies:
        copy.start()
    for k, copy in enumerate(copies):
        copy.wait()
        if scale is not None:
            outs[k][...] = (held[k] * scale).astype(outs[k].dtype)


def by_owner(array, owner_expert, scale, *later_than):
    owners = array.shape[0]
    scratch = [pltpu.SemaphoreType.DMA((owners,))]
    if scale is not None:
        scratch = [pltpu.VMEM(array.shape, array.dtype)] + scratch
    return pl.pallas_call(
        functools.partial(by_owner_kernel, owners, scale, len(later_than)),
        out_shape=[jax.ShapeDtypeStruct(array.shape[1:], jnp.bfloat16)] * owners,
        in_specs=[ANY, SMEM] + [ANY] * len(later_than),
        out_specs=[VMEM] * owners,
        scratch_shapes=scratch,
        compiler_params=pltpu.CompilerParams(vmem_limit_bytes=56 << 20),
        cost_estimate=pl.CostEstimate(
            flops=0, bytes_accessed=array.size * (array.dtype.itemsize + 2), transcendentals=0
        ),
        name="by_owner",
    )(array, owner_expert, *later_than)


def newton_kernel(chunk, owners, *rest):
    pieces, (out_ref, poly_ref) = rest[:owners], rest[-2:]
    shard, width = pieces[0].shape
    column = lax.axis_index("fsdp")
    total = jnp.float32(0.0)
    for piece in pieces:
        wide = piece[...].astype(jnp.float32)
        total += jnp.sum(wide * wide)
    scale = 1.0 / (jnp.sqrt(total) + norm_eps)
    for step, piece in enumerate(pieces):
        start = source(column, step, owners) * shard
        out_ref[pl.ds(pl.multiple_of(start, shard), shard), :] = (
            piece[...].astype(jnp.float32) * scale
        ).astype(jnp.bfloat16)

    def iteration(_, carry):
        state = out_ref[...]
        square = lax.dot_general(
            state, state, ROW_BY_ROW, preferred_element_type=jnp.float32
        ).astype(jnp.bfloat16)
        twice = jnp.dot(square, square, preferred_element_type=jnp.float32)
        poly_ref[...] = (
            quintic_two * square.astype(jnp.float32) + quintic_three * twice
        ).astype(jnp.bfloat16)

        def columns(c, carry):
            at = pl.ds(pl.multiple_of(c * chunk, chunk), chunk)
            part = out_ref[:, at]
            out_ref[:, at] = (
                quintic_one * part.astype(jnp.float32)
                + jnp.dot(poly_ref[...], part, preferred_element_type=jnp.float32)
            ).astype(jnp.bfloat16)
            return carry

        return lax.fori_loop(0, width // chunk, columns, carry)

    lax.fori_loop(0, ITERS, iteration, 0)


def orthogonalize(pieces, *later_than):
    owners = len(pieces)
    rows, width = pieces[0].shape[0] * owners, pieces[0].shape[1]
    chunk = 1024 if width % 1024 == 0 else width
    return pl.pallas_call(
        functools.partial(newton_kernel, chunk, owners),
        out_shape=jax.ShapeDtypeStruct((rows, width), jnp.bfloat16),
        in_specs=[VMEM] * owners + [ANY] * len(later_than),
        out_specs=VMEM,
        scratch_shapes=[pltpu.VMEM((rows, rows), jnp.bfloat16)],
        compiler_params=pltpu.CompilerParams(vmem_limit_bytes=56 << 20),
        cost_estimate=pl.CostEstimate(
            flops=ITERS * 2 * rows * rows * (2 * width + rows),
            bytes_accessed=4 * rows * width,
            transcendentals=0,
        ),
        name="newton",
    )(*pieces, *later_than)


def refresh_kernel(factor, owners, update_ref, *rest):
    pieces, out_ref = rest[:owners], rest[-1]
    shard = pieces[0].shape[0]
    column = lax.axis_index("fsdp")
    for step, piece in enumerate(pieces):
        at = pl.ds(pl.multiple_of(source(column, step, owners) * shard, shard), shard)
        out_ref[at, :] = (
            piece[...].astype(jnp.float32) - factor * update_ref[at, :].astype(jnp.float32)
        ).astype(jnp.bfloat16)


def refresh(update, pieces, *later_than):
    factor = learn_rate * 0.2 * math.sqrt(max(update.shape))
    return pl.pallas_call(
        functools.partial(refresh_kernel, factor, len(pieces)),
        out_shape=jax.ShapeDtypeStruct(update.shape, jnp.bfloat16),
        in_specs=[VMEM] * (1 + len(pieces)) + [ANY] * len(later_than),
        out_specs=VMEM,
        compiler_params=pltpu.CompilerParams(vmem_limit_bytes=32 << 20),
        cost_estimate=pl.CostEstimate(
            flops=2 * update.size, bytes_accessed=6 * update.size, transcendentals=0
        ),
        name="refresh",
    )(update, *pieces, *later_than)


def per_device(weights, momentum, tokens, block_expert, owner_expert):
    owners = lax.axis_size("fsdp")
    groups = lax.axis_size("replica")
    group = lax.axis_index("replica")
    blocks = block_expert.shape[0]
    width = tokens.shape[1]
    rows = weights.shape[1] * owners
    resident = tokens.reshape(blocks, -1, width)
    half = groups // 2
    places = list(range(0, groups, 2))
    teams = [[team + place for place in places] for team in (0, 1)]
    far = list(range(half + 1, groups, 2))
    near = list(range(1, half, 2))

    def at_step(step):
        return lambda: partner(lax.axis_index("replica"), step, groups)

    def at_place(place):
        return lambda: lax.axis_index("replica") % 2 + place

    arrived = {}

    def pick_and_send(steps, *later_than):
        picked = pick(
            resident, block_expert, [at_step(step) for step in steps], owners, False, *later_than
        )
        for block, step in zip(picked, steps):
            arrived[step] = send(block, "replica", step, groups)
        return picked

    def exchange(blocks):
        return lax.all_to_all(blocks, "replica", 0, 0, axis_index_groups=teams, tiled=True)

    outgoing = pick(resident, block_expert, [at_place(place) for place in places], owners, True)
    team = exchange(outgoing)
    moment = by_owner(momentum, owner_expert, None, outgoing)
    moment = [moment[0]] + [send(moment[k], "fsdp", k, owners) for k in range(1, owners)]
    pick_and_send(near, outgoing)
    sent = pick_and_send(far, *moment, arrived[near[0]])
    kept = 1.0 - learn_rate * weight_decay
    master = by_owner(weights, owner_expert, kept, *moment )
    master = [master[0]] + [send(master[k], "fsdp", k, owners) for k in range(1, owners)]
    update = orthogonalize(moment , *[arrived[step] for step in near], sent[0])
    refreshed = refresh(update, master )

    def product(block):
        return lax.dot_general(
            block, refreshed, ROW_BY_ROW, preferred_element_type=jnp.float32
        ).astype(jnp.bfloat16)

    reply = product(team.reshape(-1, width)).reshape(half, -1, rows)
    answers = [exchange(reply)]
    steps = near + far
    replies = []
    for step in steps:
        replies.append(product(after(arrived[step], reply, *replies)))
        answers.append(send_back(replies[-1], "replica", step, groups)[None])
    served = jnp.concatenate(
        [
            group % 2 + jnp.array(places, jnp.int32),
            partner(group, jnp.array(steps, jnp.int32), groups),
        ]
    )
    order = jnp.argmax((block_expert // owners)[:, None] == served[None, :], axis=1)
    rollout = jnp.take(jnp.concatenate(answers), order, axis=0, mode="clip").reshape(-1, rows)
    return (refreshed[None], rollout)


def solution(mesh):
    placed = (
        P("replica", "fsdp", None),
        P("replica", "fsdp", None),
        P(("fsdp", "replica"), None),
        P(("fsdp", "replica")),
        P(),
    )
    return jax.shard_map(
        per_device,
        mesh=mesh,
        in_specs=placed,
        out_specs=(P(("fsdp", "replica"), None, None), P(("fsdp", "replica"), None)),
        check_vma=False,
    )
```
